1024 devices in a mesh: domain: 64 (over x_hi, z, core), band: 16 (over y, x_lo).
Axes of the slice: x: 4 (x_hi: 2, x_lo: 2; x = x_hi * 2 + x_lo), y: 8, z: 16, core: 2. Of those that a mesh axis runs over, the one named last changes fastest.
Arguments:
- orbitals: float32 [64, 1024, 16, 128], P('band', 'domain'), may hold values from -50 to 50
- potential: float32 [1024, 16, 128], P('domain'), may hold values from -3 to 1
- projectors: float32 [2048, 32768], P('domain'), may hold values from -0.5 to 0.5
- slot_ids: int32 [2048], P('domain'), may hold values from 0 to 1023, as said below
- slot_count: int32 [64], P('domain'), may hold values from 16 to 32, as said below
- energies: float32 [1024], replicated, may hold values from 1 to 4
Outputs:
- filtered: float32 [64, 1024, 16, 128], P('band', 'domain')
- margin: float32 [64, 64], P('band')
The draws below stay inside these ranges and needn't reach their ends.
Inputs may be any that keep to these rules, and one draw needn't show every extreme that they name: `slot_ids`: device d owns projectors d * 16 to (d + 1) * 16 - 1. The first 16 slots of block d name its own projectors, each once; its other slots name projectors owned by blocks that share a face with it, and a projector may be named by several slots. Slots 0 to slot_count[d] - 1 of block d are live, the rest are padding; some block has all 32 slots live.
All inputs are finite; a program needn't handle non-finite values.
Results may differ from the reference program's by a relative error of at most 0.00035.
Values may be sent and summed in bfloat16 or wider, within the bound.
A program may use at most 64 MiB of HBM per device.

```python
import math
import jax
import jax.numpy as jnp
import numpy as np
from jax import lax

CX = 16
CY = 16
CZ = 128
GZ = 4
GY = 4
GX = 4
CELLS = 32768
NCELLS = 2097152
DX = 1024
PROJ_DEV = 16
PSLOT = 32
NPROJ = 1024
SLOTS = 2048
NBLOCK = 64


def draw_orbitals(key, part):
    key = jax.random.fold_in(key, 1)
    scale_key, common_key, rough_key = jax.random.split(key, 3)
    shape = (NBLOCK, DX, CY, CZ)
    scales = jnp.exp(jax.random.uniform(scale_key, (NBLOCK, 1, 1, 1), jnp.float32, -0.7, 0.7))
    shared = jax.random.truncated_normal(common_key, -4.0, 4.0, (1, DX, CY, CZ), jnp.float32)
    rough_part = jax.random.truncated_normal(rough_key, -4.0, 4.0, shape, jnp.float32)
    mixing = 0.5
    return scales * (rough_part + mixing * shared)


def gray_code(values):
    return jnp.bitwise_xor(values, values // 2)


def draw_slot_ids(key, part):
    key = jax.random.fold_in(key, 2)
    order_key, heading_key, within_key = jax.random.split(key, 3)
    devices = NPROJ // PROJ_DEV
    device_ids = jnp.arange(devices, dtype=jnp.int32)
    own_order = jax.vmap(lambda single: jax.random.permutation(single, PROJ_DEV))(jax.random.split(order_key, devices))
    own_ids = own_order.astype(jnp.int32) + device_ids[:, None] * PROJ_DEV
    extra = PSLOT - PROJ_DEV
    heading = jax.random.randint(heading_key, (devices, extra), 0, 6, dtype=jnp.int32)
    picked_axis = heading // 2
    step_size = 2 * (heading % 2) - 1
    coord_x = gray_code(device_ids[:, None] // (GY * GZ))
    coord_y = gray_code(device_ids[:, None] // GZ % GY)
    coord_z = gray_code(device_ids[:, None] % GZ)
    beside_x = gray_code((coord_x + jnp.where(picked_axis == 0, step_size, 0)) % GX)
    beside_y = gray_code((coord_y + jnp.where(picked_axis == 1, step_size, 0)) % GY)
    beside_z = gray_code((coord_z + jnp.where(picked_axis == 2, step_size, 0)) % GZ)
    neighbour = (beside_x * GY + beside_y) * GZ + beside_z
    within = jax.random.randint(within_key, (devices, extra), 0, PROJ_DEV, dtype=jnp.int32)
    result = jnp.concatenate([own_ids, neighbour * PROJ_DEV + within], axis=1)
    return result.reshape(-1).astype(jnp.int32)


def draw_slot_count(key, part):
    key = jax.random.fold_in(key, 3)
    count_key, pick_key = jax.random.split(key, 2)
    devices = NPROJ // PROJ_DEV
    device_ids = jnp.arange(devices, dtype=jnp.int32)
    counts = jax.random.randint(count_key, (devices,), PROJ_DEV, PSLOT + 1, dtype=jnp.int32)
    chosen = jax.random.randint(pick_key, (), 0, devices, dtype=jnp.int32)
    return jnp.where(device_ids == chosen, PSLOT, counts).astype(jnp.int32)


def block_scale(stream_key, dims, pieces, least, high):
    def one(dim, blocks):
        heights = jax.random.uniform(jax.random.fold_in(jax.random.fold_in(stream_key, 6), dim), (blocks,), jnp.float32, least / len(pieces), high / len(pieces))
        return jnp.repeat(jnp.exp(heights), dims[dim] // blocks).reshape((-1,) + (1,) * (len(dims) - dim - 1))

    factor_of = one(*pieces[0])
    for cut in pieces[1:]:
        factor_of = factor_of * one(*cut)
    return factor_of


def noise(key, shape, scale, reach, cuts=(), kind=jnp.bfloat16):
    drawn = scale * jax.random.normal(key, shape, jnp.float32)
    if cuts:
        drawn = drawn * block_scale(key, shape, cuts, -0.22, 0.18)
    return jnp.clip(drawn, -reach, reach).astype(kind)


def setup_inputs(seed: int = 0) -> dict:
    seeds = jax.random.split(jax.random.key(seed), 7)
    orbitals = draw_orbitals(jax.random.fold_in(seeds[6], 71), 0)
    potential = jnp.clip(-3.0 + 4.0 * jax.random.uniform(seeds[1], (DX, CY, CZ), jnp.float32) ** block_scale(seeds[1], (DX, CY, CZ), ((0, 64),), -0.2, 0.2), -3.0, 1.0)
    projectors = noise(seeds[2], (SLOTS, CELLS), ((PSLOT * CELLS) ** -0.25), 0.5, ((0, 64),), jnp.float32)
    slot_ids = draw_slot_ids(jax.random.fold_in(seeds[6], 71), 0)
    slot_count = draw_slot_count(jax.random.fold_in(seeds[6], 71), 0)
    energies = jnp.clip(jnp.exp(jax.random.uniform(seeds[5], (NPROJ,), jnp.float32, math.log(1.0), math.log(4.0))), 1.0, 4.0)
    return {"orbitals": orbitals, "potential": potential, "projectors": projectors, "slot_ids": slot_ids, "slot_count": slot_count, "energies": energies}


STENCIL = (-5369.0 / 1800.0, 12.0 / 7.0, -15.0 / 56.0, 10.0 / 189.0, -1.0 / 112.0, 2.0 / 1925.0, -1.0 / 16632.0)
SPACING = 0.5
CENTER = 27.5
HALF_WIDTH = 22.5


def gray_order(count):
    return np.array([value ^ (value >> 1) for value in range(count)], dtype=np.int32)


def reorder(shaped, axes_counts):
    for position, count in axes_counts:
        shaped = jnp.take(shaped, gray_order(count), axis=position)
    return shaped


def to_grid(blocks):
    orbital_rows = blocks.shape[0]
    shaped = blocks.reshape(orbital_rows, GX, GY, GZ, CX, CY, CZ)
    shaped = reorder(shaped, ((1, GX), (2, GY), (3, GZ)))
    return shaped.transpose(0, 1, 4, 2, 5, 3, 6).reshape(orbital_rows, GX * CX, GY * CY, GZ * CZ)


def to_blocks(values):
    orbital_rows = values.shape[0]
    shaped = values.reshape(orbital_rows, GX, CX, GY, CY, GZ, CZ)
    shaped = reorder(shaped, ((1, GX), (3, GY), (5, GZ)))
    return shaped.transpose(0, 1, 3, 5, 2, 4, 6).reshape(orbital_rows, GX * GY * GZ * CX, CY, CZ)


def kinetic_single(values):
    summed = (3.0 * STENCIL[0]) * values
    for dimension in (0, 1, 2):
        for offset in range(1, len(STENCIL)):
            summed = summed + STENCIL[offset] * (jnp.roll(values, offset, dimension) + jnp.roll(values, -offset, dimension))
    return (-0.5 / (SPACING * SPACING)) * summed


def nonlocal_term(blocks, projectors, slot_ids, slot_count, energies):
    orbital_rows = blocks.shape[0]
    domains = slot_count.shape[0]
    flattened = blocks.reshape(orbital_rows, domains, CELLS)
    shaped_proj = projectors.reshape(domains, PSLOT, CELLS)
    active_slots = (jnp.arange(PSLOT)[None, :] < slot_count[:, None]).astype(flattened.dtype)
    partial_value = jnp.einsum('dsc,bdc->bds', shaped_proj, flattened, precision=lax.Precision.HIGHEST) * active_slots[None]
    coefficient = jnp.zeros((orbital_rows, NPROJ), flattened.dtype).at[:, slot_ids].add(partial_value.reshape(orbital_rows, -1))
    weights = coefficient[:, slot_ids] * energies[slot_ids][None, :]
    weights = weights.reshape(orbital_rows, domains, PSLOT) * active_slots[None]
    term = jnp.einsum('bds,dsc->bdc', weights, shaped_proj, precision=lax.Precision.HIGHEST)
    return term.reshape(blocks.shape)


def reference(orbitals, potential, projectors, slot_ids, slot_count, energies):
    def hamiltonian(values):
        kinetic = to_blocks(lax.map(kinetic_single, to_grid(values)))
        return kinetic + potential[None] * values + nonlocal_term(values, projectors, slot_ids, slot_count, energies)

    first = (hamiltonian(orbitals) - CENTER * orbitals) / HALF_WIDTH
    filtered = 2.0 * (hamiltonian(first) - CENTER * first) / HALF_WIDTH - orbitals
    rounded = filtered.astype(jnp.bfloat16).reshape(filtered.shape[0], -1)
    margin = jnp.dot(rounded, rounded.T, preferred_element_type=jnp.float32) / NCELLS
    return (filtered, margin)
```

```python
import jax
import jax.numpy as jnp
from jax import lax
from jax.experimental import pallas as pl
from jax.experimental.pallas import tpu as pltpu
from jax.sharding import PartitionSpec as P

STENCIL = (
    -5369.0 / 1800.0,
    12.0 / 7.0,
    -15.0 / 56.0,
    10.0 / 189.0,
    -1.0 / 112.0,
    2.0 / 1925.0,
    -1.0 / 16632.0,
)
SPACING = 0.5
CENTER = 27.5
HALF_WIDTH = 22.5
RADIUS = 6
ORBS = 4
SLOTS = 32
CELLROWS = 256
PADROWS = 448
LOW = 96
DOMAINS = 64
BANDS = 16
NCELLS = 2097152

SCALE = -0.5 / (SPACING * SPACING) / HALF_WIDTH
COEF = [SCALE * c for c in STENCIL]
MESH = pl.DeviceIdType.MESH


def neighbours(d):
    found = []
    for low in (16, 4, 1):
        first, second = d // low % 2, d // (2 * low) % 2
        by_first = d + low * (1 - 2 * first)
        by_second = d + 2 * low * (1 - 2 * second)
        lead = 1 - (first + second) % 2
        found.append(lead * by_first + (1 - lead) * by_second)
        found.append(lead * by_second + (1 - lead) * by_first)
    return found


def split(value):
    high = value.astype(jnp.bfloat16)
    low = (value - high.astype(jnp.float32)).astype(jnp.bfloat16)
    return high, low


def dot_nt(left, right):
    return lax.dot_general(
        left, right, (((1,), (1,)), ((), ())), preferred_element_type=jnp.float32
    )


def dot_tn(left, right):
    return lax.dot_general(
        left, right, (((0,), (0,)), ((), ())), preferred_element_type=jnp.float32
    )


def filter_kernel(
    ids_ref,
    count_ref,
    energies_ref,
    orb_ref,
    pot_ref,
    proj_ref,
    filt_ref,
    round_ref,
    field,
    turned,
    proj,
    proj_rows,
    diag,
    face_send,
    face_recv,
    edge_send,
    edge_recv,
    coef_send,
    coef_recv,
    band_matrix,
    edge_matrix,
    pick_matrix,
    selector,
    splat,
    term_y,
    term_z,
    in_sem,
    halo_send_sem,
    halo_recv_sem,
    coef_send_sem,
    coef_recv_sem,
):
    d = lax.axis_index("domain")
    b = lax.axis_index("band")
    near = neighbours(d)

    loads = [
        pltpu.make_async_copy(
            orb_ref.at[pl.ds(o * CELLROWS, CELLROWS)],
            field.at[0, o, pl.ds(LOW, CELLROWS)],
            in_sem.at[o],
        )
        for o in range(ORBS)
    ]
    loads.append(pltpu.make_async_copy(proj_ref, proj, in_sem.at[ORBS]))
    loads.append(pltpu.make_async_copy(pot_ref, diag, in_sem.at[ORBS + 1]))
    for load in loads:
        load.start()

    barrier = pltpu.get_barrier_semaphore()
    for k in range(6):
        pl.semaphore_signal(barrier, inc=1, device_id=(near[k], b), device_id_type=MESH)

    rows = lax.broadcasted_iota(jnp.int32, (128, 128), 0)
    lanes = lax.broadcasted_iota(jnp.int32, (128, 128), 1)
    apart = jnp.abs(rows - lanes)
    banded = jnp.zeros((128, 128), jnp.float32)
    for k in range(1, RADIUS + 1):
        banded = jnp.where(apart == k, COEF[k], banded)
    high, low = split(banded)
    band_matrix[0:128, 0:128] = high
    band_matrix[128:256, 0:128] = high
    band_matrix[0:128, 128:256] = low
    band_matrix[128:256, 128:256] = low

    rows = lax.broadcasted_iota(jnp.int32, (32, 128), 0)
    lanes = lax.broadcasted_iota(jnp.int32, (32, 128), 1)
    layer = rows & 7
    half = (rows >> 3) & 1
    side = rows >> 4
    used = layer < RADIUS
    reach = jnp.where(side == 0, lanes + RADIUS - layer, 128 + layer - lanes)
    edge = jnp.zeros((32, 128), jnp.float32)
    for k in range(1, RADIUS + 1):
        edge = jnp.where(reach == k, COEF[k], edge)
    edge = jnp.where(used, edge, 0.0)
    picked = jnp.where(side == 0, 128 - RADIUS + layer, layer)
    pick = jnp.where(used, jnp.where(lanes == picked, 1.0, 0.0), 0.0)
    for part in range(2):
        high, low = split(jnp.where(half == part, edge, 0.0))
        edge_matrix[:, 256 * part : 256 * part + 128] = high
        edge_matrix[:, 256 * part + 128 : 256 * part + 256] = low
        pick_matrix[:, 128 * part : 128 * part + 128] = jnp.where(half == part, pick, 0.0).astype(
            jnp.bfloat16
        )

    lane = lax.broadcasted_iota(jnp.int32, (1, 128), 1)
    group = lane >> 4
    target = jnp.full((1, 128), -(2**20), jnp.int32)
    for g, block in enumerate(near + [d]):
        target = jnp.where(group == g, block * 16 + (lane & 15), target)
    live = count_ref[0]
    for s in range(SLOTS):
        named = jnp.where(s < live, ids_ref[s], -1)
        selector[s : s + 1, :] = jnp.where(target == named, 1.0, 0.0)
    own_energy = energies_ref[pl.ds(d // 8, 1), :]
    own_energy = pltpu.roll(own_energy, (128 - d % 8 * 16) % 128, 1)
    own_energy = jnp.where(lane < 16, own_energy / HALF_WIDTH, 0.0)

    def halo_copy(h, o, k):
        if k < 4:
            src, dst = face_send.at[h, o, k], face_recv.at[h, o, k ^ 1]
        else:
            src, dst = edge_send.at[h, o, k - 4], edge_recv.at[h, o, (k ^ 1) - 4]
        return pltpu.make_async_remote_copy(
            src_ref=src,
            dst_ref=dst,
            send_sem=halo_send_sem.at[h, o, k],
            recv_sem=halo_recv_sem.at[h, o, k ^ 1],
            device_id=(near[k], b),
            device_id_type=MESH,
        )

    def send_halo(h, o):
        for k in range(6):
            halo_copy(h, o, k).start()

    def coef_copy(h, turn, k):
        return pltpu.make_async_remote_copy(
            src_ref=coef_send.at[h, turn],
            dst_ref=coef_recv.at[h, turn, k ^ 1],
            send_sem=coef_send_sem.at[h, turn, k],
            recv_sem=coef_recv_sem.at[h, turn, k ^ 1],
            device_id=(near[k], b),
            device_id_type=MESH,
        )

    def prepare(h, o):
        face_send[h, o, 0] = field[h, o, pl.ds(LOW + 160, LOW), :].astype(jnp.bfloat16)
        face_send[h, o, 1] = field[h, o, pl.ds(LOW, LOW), :].astype(jnp.bfloat16)
        for y in range(16):
            layer = field[h, o, pl.ds(LOW + y, 16, stride=16), :]
            turned[o, pl.ds(LOW + 16 * y, 16), :] = layer
            if y >= 10:
                face_send[h, o, 2, pl.ds(16 * (y - 10), 16), :] = layer.astype(jnp.bfloat16)
            if y < RADIUS:
                face_send[h, o, 3, pl.ds(16 * y, 16), :] = layer.astype(jnp.bfloat16)
        first_half = field[h, o, pl.ds(LOW, 128), :].astype(jnp.bfloat16)
        second_half = field[h, o, pl.ds(LOW + 128, 128), :].astype(jnp.bfloat16)
        edges = dot_nt(pick_matrix[:, 0:128], first_half) + dot_nt(
            pick_matrix[:, 128:256], second_half
        )
        edge_send[h, o, 0] = edges[0:16].astype(jnp.bfloat16)
        edge_send[h, o, 1] = edges[16:32].astype(jnp.bfloat16)

    def project(h):
        def body(x, sums):
            sums = list(sums)
            for y in range(16):
                row = x * 16 + y
                columns = proj[:, pl.ds(pl.multiple_of(row * 128, 128), 128)]
                for o in range(ORBS):
                    sums[o] = sums[o] + columns * field[h, o, pl.ds(LOW + row, 1), :]
            return tuple(sums)

        zero = jnp.zeros((SLOTS, 128), jnp.float32)
        sums = lax.fori_loop(0, 16, body, (zero,) * ORBS)
        chosen = selector[...]
        for o in range(ORBS):
            partial = jnp.sum(sums[o], axis=1, keepdims=True)
            coef_send[h, 0, o : o + 1, :] = jnp.sum(partial * chosen, axis=0, keepdims=True)
        for k in range(6):
            coef_copy(h, 0, k).start()

    def own_coefficients(h):
        for k in range(6):
            coef_copy(h, 0, k).wait_recv()
        total = pltpu.roll(coef_send[h, 0], 32, 1)
        for k in range(6):
            total = total + pltpu.roll(coef_recv[h, 0, k], (128 - 16 * (k ^ 1)) % 128, 1)
        coef_send[h, 1] = total * own_energy
        for k in range(6):
            coef_copy(h, 1, k).start()

    def weigh(h):
        for k in range(6):
            coef_copy(h, 1, k).wait_recv()
        known = pltpu.roll(coef_send[h, 1], 96, 1)
        for k in range(6):
            known = known + pltpu.roll(coef_recv[h, 1, k], 16 * k, 1)
        chosen = selector[...]
        for o in range(ORBS):
            weight = jnp.sum(chosen * known[o : o + 1, :], axis=1, keepdims=True)
            splat[o * SLOTS : (o + 1) * SLOTS, :] = jnp.broadcast_to(weight, (SLOTS, 128))

    def apply(h, o):
        for k in range(6):
            halo_copy(h, o, k).wait_recv()
        field[h, o, pl.ds(LOW + CELLROWS, LOW), :] = face_recv[h, o, 0].astype(jnp.float32)
        field[h, o, pl.ds(0, LOW), :] = face_recv[h, o, 1].astype(jnp.float32)
        turned[o, pl.ds(LOW + CELLROWS, LOW), :] = face_recv[h, o, 2].astype(jnp.float32)
        turned[o, pl.ds(0, LOW), :] = face_recv[h, o, 3].astype(jnp.float32)

        high, low = split(field[h, o, pl.ds(LOW, CELLROWS), :])
        along = jnp.dot(
            jnp.concatenate([high, low], axis=1),
            band_matrix[...],
            preferred_element_type=jnp.float32,
        )
        along = along[:, 0:128] + along[:, 128:256]
        ends = dot_tn(
            jnp.concatenate([edge_recv[h, o, 1], edge_recv[h, o, 0]], axis=0), edge_matrix[...]
        )
        term_z[0:128, :] = along[0:128] + (ends[:, 0:128] + ends[:, 128:256])
        term_z[128:256, :] = along[128:256] + (ends[:, 256:384] + ends[:, 384:512])

        def body_y(y, carry):
            total = jnp.zeros((64, 128), jnp.float32)
            for k in range(1, RADIUS + 1):
                total = total + COEF[k] * (
                    turned[o, pl.ds(LOW + 64 * y + 16 * k, 64), :]
                    + turned[o, pl.ds(LOW + 64 * y - 16 * k, 64), :]
                )
            term_y[pl.ds(64 * y, 64), :] = total
            return carry

        lax.fori_loop(0, 4, body_y, 0)

        def body_x(x, carry):
            here = pl.ds(64 * x, 64)
            value = field[h, o, pl.ds(LOW + 64 * x, 64), :]
            total = diag[here, :] * value + term_z[here, :]
            total = total + jnp.concatenate(
                [term_y[pl.ds(4 * x + i, 16, stride=16), :] for i in range(4)], axis=0
            )
            for k in range(1, RADIUS + 1):
                total = total + COEF[k] * (
                    field[h, o, pl.ds(LOW + 64 * x + 16 * k, 64), :]
                    + field[h, o, pl.ds(LOW + 64 * x - 16 * k, 64), :]
                )
            for s in range(SLOTS):
                total = total + splat[pl.ds(o * SLOTS + s, 1), :] * proj_rows[
                    pl.ds(s * CELLROWS + 64 * x, 64), :
                ]
            if h == 0:
                field[1, o, pl.ds(LOW + 64 * x, 64), :] = total
            else:
                total = 2.0 * total - field[0, o, pl.ds(LOW + 64 * x, 64), :]
                place = pl.ds(o * CELLROWS + 64 * x, 64)
                filt_ref[place, :] = total
                round_ref[place, :] = total.astype(jnp.bfloat16)
            return carry

        lax.fori_loop(0, 4, body_x, 0)

    def over_orbitals(body, first=0, last=ORBS):
        lax.fori_loop(first, last, lambda o, carry: (body(o), carry)[1], 0)

    for o in range(ORBS):
        loads[o].wait()
    over_orbitals(lambda o: prepare(0, o))
    pl.semaphore_wait(barrier, 6)
    send_halo(0, 0)
    loads[ORBS].wait()
    project(0)
    send_halo(0, 1)

    def turn(row, carry):
        proj_rows[pl.ds(row, SLOTS, stride=CELLROWS), :] = proj[
            :, pl.ds(pl.multiple_of(row * 128, 128), 128)
        ]
        return carry

    lax.fori_loop(0, CELLROWS, turn, 0, unroll=8)
    loads[ORBS + 1].wait()
    diag[...] = (diag[...] + (-0.5 / (SPACING * SPACING) * 3.0 * STENCIL[0] - CENTER)) * (
        1.0 / HALF_WIDTH
    )
    own_coefficients(0)
    send_halo(0, 2)
    send_halo(0, 3)
    weigh(0)

    def first_step(o):
        apply(0, o)
        prepare(1, o)

    def first_step_and_send(o):
        first_step(o)
        send_halo(1, o)

    over_orbitals(first_step_and_send, 0, 2)
    over_orbitals(first_step, 2, 4)
    project(1)
    send_halo(1, 2)
    own_coefficients(1)
    send_halo(1, 3)
    weigh(1)
    over_orbitals(lambda o: apply(1, o))

    for h in range(2):
        for turn_ in range(2):
            for k in range(6):
                coef_copy(h, turn_, k).wait_send()

        def sent(o):
            for k in range(6):
                halo_copy(h, o, k).wait_send()

        over_orbitals(sent)


def margin_kernel(
    round_ref,
    margin_ref,
    cells,
    wide,
    shares,
    gathered,
    group_low,
    group_high,
    cell_send_sem,
    cell_recv_sem,
    share_send_sem,
    share_recv_sem,
    low_send_sem,
    low_recv_sem,
    high_send_sem,
    high_recv_sem,
):
    d = lax.axis_index("domain")
    b = lax.axis_index("band")
    d_low, d_high = d % 8, d // 8

    def band_peer(i):
        return (b + i) % BANDS

    def low_peer(i):
        return d_high * 8 + (d_low + i) % 8

    def high_peer(i):
        return (d_high + i) % 8 * 8 + d_low

    def each(first, last, body):
        lax.fori_loop(first, last, lambda i, carry: (body(i), carry)[1], 0)

    barrier = pltpu.get_barrier_semaphore()

    def greet_band(i):
        pl.semaphore_signal(barrier, inc=1, device_id=(d, band_peer(i)), device_id_type=MESH)

    def greet_domain(i):
        pl.semaphore_signal(barrier, inc=1, device_id=(low_peer(i), b), device_id_type=MESH)
        pl.semaphore_signal(barrier, inc=1, device_id=(high_peer(i), b), device_id_type=MESH)

    each(1, BANDS, greet_band)
    each(1, 8, greet_domain)
    cells[b] = round_ref[:, b]
    pl.semaphore_wait(barrier, BANDS - 1 + 14)

    def cell_copy(i):
        return pltpu.make_async_remote_copy(
            src_ref=round_ref.at[:, band_peer(i)],
            dst_ref=cells.at[b],
            send_sem=cell_send_sem.at[i],
            recv_sem=cell_recv_sem.at[i],
            device_id=(d, band_peer(i)),
            device_id_type=MESH,
        )

    def share_copy(i):
        return pltpu.make_async_remote_copy(
            src_ref=shares.at[band_peer(i)],
            dst_ref=gathered.at[b],
            send_sem=share_send_sem.at[i],
            recv_sem=share_recv_sem.at[i],
            device_id=(d, band_peer(i)),
            device_id_type=MESH,
        )

    def low_copy(i):
        return pltpu.make_async_remote_copy(
            src_ref=group_low.at[d_low],
            dst_ref=group_low.at[d_low],
            send_sem=low_send_sem.at[i],
            recv_sem=low_recv_sem.at[i],
            device_id=(low_peer(i), b),
            device_id_type=MESH,
        )

    def high_copy(i):
        return pltpu.make_async_remote_copy(
            src_ref=group_high.at[d_high],
            dst_ref=group_high.at[d_high],
            send_sem=high_send_sem.at[i],
            recv_sem=high_recv_sem.at[i],
            device_id=(high_peer(i), b),
            device_id_type=MESH,
        )

    each(1, BANDS, lambda i: cell_copy(i).start())
    each(1, BANDS, lambda i: cell_copy(i).wait_recv())

    def widen(j, carry):
        for o in range(ORBS):
            wide[pl.ds(j * 64 + o * 16, 16), :] = cells[j, o].astype(jnp.float32)
        return carry

    lax.fori_loop(0, BANDS, widen, 0)
    gram = jnp.zeros((64, 64), jnp.float32)
    for row in range(0, 16, 2):
        part = jnp.concatenate(
            [wide[pl.ds(row + i, 64, stride=16), :] for i in range(2)], axis=1
        ).astype(jnp.bfloat16)
        gram = gram + dot_nt(part, part)
    gram = jnp.concatenate([gram, jnp.zeros((64, 64), jnp.float32)], axis=1)
    for j in range(BANDS):
        shares[j] = gram[ORBS * j : ORBS * (j + 1), :]
    each(1, BANDS, lambda i: share_copy(i).start())
    gathered[b] = shares[b]
    each(1, BANDS, lambda i: share_copy(i).wait_recv())
    total = gathered[0]
    for j in range(1, BANDS):
        total = total + gathered[j]
    group_low[d_low] = total
    each(1, 8, lambda i: low_copy(i).start())
    each(1, 8, lambda i: low_copy(i).wait_recv())
    total = group_low[0]
    for j in range(1, 8):
        total = total + group_low[j]
    group_high[d_high] = total
    each(1, 8, lambda i: high_copy(i).start())
    each(1, 8, lambda i: high_copy(i).wait_recv())
    total = group_high[0]
    for j in range(1, 8):
        total = total + group_high[j]
    margin_ref[...] = total[:, 0:64] * (1.0 / NCELLS)

    each(1, BANDS, lambda i: cell_copy(i).wait_send())
    each(1, BANDS, lambda i: share_copy(i).wait_send())
    each(1, 8, lambda i: low_copy(i).wait_send())
    each(1, 8, lambda i: high_copy(i).wait_send())


def on_device(orbitals, potential, projectors, slot_ids, slot_count, energies):
    vmem = pl.BlockSpec(memory_space=pltpu.VMEM)
    smem = pl.BlockSpec(memory_space=pltpu.SMEM)
    anywhere = pl.BlockSpec(memory_space=pl.ANY)
    filtered, rounded = pl.pallas_call(
        filter_kernel,
        out_shape=(
            jax.ShapeDtypeStruct((ORBS * CELLROWS, 128), jnp.float32),
            jax.ShapeDtypeStruct((ORBS * CELLROWS, 128), jnp.bfloat16),
        ),
        in_specs=[smem, smem, vmem, anywhere, anywhere, anywhere],
        out_specs=(vmem, vmem),
        scratch_shapes=[
            pltpu.VMEM((2, ORBS, PADROWS, 128), jnp.float32),
            pltpu.VMEM((ORBS, PADROWS, 128), jnp.float32),
            pltpu.VMEM((SLOTS, 32768), jnp.float32),
            pltpu.VMEM((SLOTS * CELLROWS, 128), jnp.float32),
            pltpu.VMEM((CELLROWS, 128), jnp.float32),
            pltpu.VMEM((2, ORBS, 4, LOW, 128), jnp.bfloat16),
            pltpu.VMEM((2, ORBS, 4, LOW, 128), jnp.bfloat16),
            pltpu.VMEM((2, ORBS, 2, 16, 128), jnp.bfloat16),
            pltpu.VMEM((2, ORBS, 2, 16, 128), jnp.bfloat16),
            pltpu.VMEM((2, 2, ORBS, 128), jnp.float32),
            pltpu.VMEM((2, 2, 6, ORBS, 128), jnp.float32),
            pltpu.VMEM((256, 256), jnp.bfloat16),
            pltpu.VMEM((32, 512), jnp.bfloat16),
            pltpu.VMEM((32, 256), jnp.bfloat16),
            pltpu.VMEM((SLOTS, 128), jnp.float32),
            pltpu.VMEM((ORBS * SLOTS, 128), jnp.float32),
            pltpu.VMEM((CELLROWS, 128), jnp.float32),
            pltpu.VMEM((CELLROWS, 128), jnp.float32),
            pltpu.SemaphoreType.DMA((ORBS + 2,)),
            pltpu.SemaphoreType.DMA((2, ORBS, 6)),
            pltpu.SemaphoreType.DMA((2, ORBS, 6)),
            pltpu.SemaphoreType.DMA((2, 2, 6)),
            pltpu.SemaphoreType.DMA((2, 2, 6)),
        ],
        compiler_params=pltpu.CompilerParams(
            collective_id=0, has_side_effects=True, vmem_limit_bytes=40 * 2**20
        ),
        name="filter",
    )(
        slot_ids,
        slot_count,
        energies.reshape(8, 128),
        orbitals.reshape(ORBS * CELLROWS, 128),
        potential.reshape(CELLROWS, 128),
        projectors,
    )
    margin = pl.pallas_call(
        margin_kernel,
        out_shape=jax.ShapeDtypeStruct((ORBS, 64), jnp.float32),
        in_specs=[vmem],
        out_specs=vmem,
        scratch_shapes=[
            pltpu.VMEM((BANDS, ORBS, 16, 128), jnp.bfloat16),
            pltpu.VMEM((64 * 16, 128), jnp.float32),
            pltpu.VMEM((BANDS, ORBS, 128), jnp.float32),
            pltpu.VMEM((BANDS, ORBS, 128), jnp.float32),
            pltpu.VMEM((8, ORBS, 128), jnp.float32),
            pltpu.VMEM((8, ORBS, 128), jnp.float32),
            pltpu.SemaphoreType.DMA((BANDS,)),
            pltpu.SemaphoreType.DMA((BANDS,)),
            pltpu.SemaphoreType.DMA((BANDS,)),
            pltpu.SemaphoreType.DMA((BANDS,)),
            pltpu.SemaphoreType.DMA((8,)),
            pltpu.SemaphoreType.DMA((8,)),
            pltpu.SemaphoreType.DMA((8,)),
            pltpu.SemaphoreType.DMA((8,)),
        ],
        compiler_params=pltpu.CompilerParams(
            collective_id=1, has_side_effects=True, vmem_limit_bytes=16 * 2**20
        ),
        name="margin",
    )(rounded.reshape(ORBS, BANDS, 16, 128))
    return filtered.reshape(orbitals.shape), margin


def solution(mesh):
    in_specs = (
        P("band", "domain", None, None),
        P("domain", None, None),
        P("domain", None),
        P("domain"),
        P("domain"),
        P(),
    )
    out_specs = (P("band", "domain", None, None), P("band", None))
    return jax.shard_map(
        on_device, mesh=mesh, in_specs=in_specs, out_specs=out_specs, check_vma=False
    )
```

```python
import jax
import jax.numpy as jnp
from jax import lax
from jax.experimental import pallas as pl
from jax.experimental.pallas import tpu as pltpu
from jax.sharding import PartitionSpec as P

STENCIL = (
    -5369.0 / 1800.0,
    12.0 / 7.0,
    -15.0 / 56.0,
    10.0 / 189.0,
    -1.0 / 112.0,
    2.0 / 1925.0,
    -1.0 / 16632.0,
)
SPACING = 0.5
CENTER = 27.5
HALF_WIDTH = 22.5
RADIUS = 6
ORBS = 4
SLOTS = 32
CELLROWS = 256
PADROWS = 448
LOW = 96
DOMAINS = 64
BANDS = 16
NCELLS = 2097152

SCALE = -0.5 / (SPACING * SPACING) / HALF_WIDTH
COEF = [SCALE * c for c in STENCIL]
MESH = pl.DeviceIdType.MESH


def neighbours(d):
    found = []
    for low in (16, 4, 1):
        first, second = d // low % 2, d // (2 * low) % 2
        by_first = d + low * (1 - 2 * first)
        by_second = d + 2 * low * (1 - 2 * second)
        lead = 1 - (first + second) % 2
        found.append(lead * by_first + (1 - lead) * by_second)
        found.append(lead * by_second + (1 - lead) * by_first)
    return found


def split(value):
    high = value.astype(jnp.bfloat16)
    low = (value - high.astype(jnp.float32)).astype(jnp.bfloat16)
    return high, low


def dot_nt(left, right):
    return lax.dot_general(
        left, right, (((1,), (1,)), ((), ())), preferred_element_type=jnp.float32
    )


def dot_tn(left, right):
    return lax.dot_general(
        left, right, (((0,), (0,)), ((), ())), preferred_element_type=jnp.float32
    )


def kernel(
    ids_ref,
    count_ref,
    energies_hbm,
    orb_ref,
    pot_ref,
    proj_ref,
    filt_hbm,
    margin_ref,
    energies_ref,
    field,
    turned,
    proj,
    proj_rows,
    diag,
    face_send,
    face_recv,
    edge_send,
    edge_recv,
    coef_send,
    coef_recv,
    band_matrix,
    edge_matrix,
    pick_matrix,
    selector,
    splat,
    term_y,
    term_z,
    filtered,
    rounded,
    cells,
    wide,
    shares,
    gathered,
    group_low,
    group_high,
    in_sem,
    out_sem,
    halo_send_sem,
    halo_recv_sem,
    coef_send_sem,
    coef_recv_sem,
    cell_send_sem,
    cell_recv_sem,
    share_send_sem,
    share_recv_sem,
    low_send_sem,
    low_recv_sem,
    high_send_sem,
    high_recv_sem,
):
    d = lax.axis_index("domain")
    b = lax.axis_index("band")
    near = neighbours(d)

    loads = [
        pltpu.make_async_copy(
            orb_ref.at[pl.ds(o * CELLROWS, CELLROWS)],
            field.at[0, o, pl.ds(LOW, CELLROWS)],
            in_sem.at[o],
        )
        for o in range(ORBS)
    ]
    loads.append(pltpu.make_async_copy(proj_ref, proj, in_sem.at[ORBS]))
    loads.append(pltpu.make_async_copy(pot_ref, diag, in_sem.at[ORBS + 1]))
    loads.append(pltpu.make_async_copy(energies_hbm, energies_ref, in_sem.at[ORBS + 2]))

    d_low, d_high = d % 8, d // 8

    def band_peer(i):
        return (b + i) % BANDS

    def low_peer(i):
        return d_high * 8 + (d_low + i) % 8

    def high_peer(i):
        return (d_high + i) % 8 * 8 + d_low

    def each(first, last, body):
        lax.fori_loop(first, last, lambda i, carry: (body(i), carry)[1], 0)

    barrier = pltpu.get_barrier_semaphore()

    def greet_band(i):
        pl.semaphore_signal(barrier, inc=1, device_id=(d, band_peer(i)), device_id_type=MESH)

    def greet_domain(i):
        pl.semaphore_signal(barrier, inc=1, device_id=(high_peer(i), b), device_id_type=MESH)
        pl.semaphore_signal(barrier, inc=1, device_id=(low_peer(i), b), device_id_type=MESH)

    each(1, 8, greet_domain)
    each(1, BANDS, greet_band)
    for load in loads:
        load.start()

    rows = lax.broadcasted_iota(jnp.int32, (128, 128), 0)
    lanes = lax.broadcasted_iota(jnp.int32, (128, 128), 1)
    apart = jnp.abs(rows - lanes)
    banded = jnp.zeros((128, 128), jnp.float32)
    for k in range(1, RADIUS + 1):
        banded = jnp.where(apart == k, COEF[k], banded)
    high, low = split(banded)
    band_matrix[0:128, 0:128] = high
    band_matrix[128:256, 0:128] = high
    band_matrix[0:128, 128:256] = low
    band_matrix[128:256, 128:256] = low

    rows = lax.broadcasted_iota(jnp.int32, (32, 128), 0)
    lanes = lax.broadcasted_iota(jnp.int32, (32, 128), 1)
    layer = rows & 7
    half = (rows >> 3) & 1
    side = rows >> 4
    used = layer < RADIUS
    reach = jnp.where(side == 0, lanes + RADIUS - layer, 128 + layer - lanes)
    edge = jnp.zeros((32, 128), jnp.float32)
    for k in range(1, RADIUS + 1):
        edge = jnp.where(reach == k, COEF[k], edge)
    edge = jnp.where(used, edge, 0.0)
    picked = jnp.where(side == 0, 128 - RADIUS + layer, layer)
    pick = jnp.where(used, jnp.where(lanes == picked, 1.0, 0.0), 0.0)
    for part in range(2):
        high, low = split(jnp.where(half == part, edge, 0.0))
        edge_matrix[:, 256 * part : 256 * part + 128] = high
        edge_matrix[:, 256 * part + 128 : 256 * part + 256] = low
        pick_matrix[:, 128 * part : 128 * part + 128] = jnp.where(half == part, pick, 0.0).astype(
            jnp.bfloat16
        )

    lane = lax.broadcasted_iota(jnp.int32, (1, 128), 1)
    group = lane >> 4
    target = jnp.full((1, 128), -(2**20), jnp.int32)
    for g, block in enumerate(near + [d]):
        target = jnp.where(group == g, block * 16 + (lane & 15), target)
    live = count_ref[0]
    for s in range(SLOTS):
        named = jnp.where(s < live, ids_ref[s], -1)
        selector[s : s + 1, :] = jnp.where(target == named, 1.0, 0.0)
    loads[ORBS + 2].wait()
    own_energy = energies_ref[pl.ds(d // 8, 1), :]
    own_energy = pltpu.roll(own_energy, (128 - d % 8 * 16) % 128, 1)
    own_energy = jnp.where(lane < 16, own_energy / HALF_WIDTH, 0.0)

    def halo_copy(h, o, k):
        if k < 4:
            src, dst = face_send.at[h, o, k], face_recv.at[h, o, k ^ 1]
        else:
            src, dst = edge_send.at[h, o, k - 4], edge_recv.at[h, o, (k ^ 1) - 4]
        return pltpu.make_async_remote_copy(
            src_ref=src,
            dst_ref=dst,
            send_sem=halo_send_sem.at[h, o, k],
            recv_sem=halo_recv_sem.at[h, o, k ^ 1],
            device_id=(near[k], b),
            device_id_type=MESH,
        )

    def send_halo(h, o):
        for k in range(6):
            halo_copy(h, o, k).start()

    def coef_copy(batch, turn, k):
        return pltpu.make_async_remote_copy(
            src_ref=coef_send.at[batch, turn],
            dst_ref=coef_recv.at[batch, turn, k ^ 1],
            send_sem=coef_send_sem.at[batch, turn, k],
            recv_sem=coef_recv_sem.at[batch, turn, k ^ 1],
            device_id=(near[k], b),
            device_id_type=MESH,
        )

    def prepare(h, o):
        face_send[h, o, 0] = field[h, o, pl.ds(LOW + 160, LOW), :].astype(jnp.bfloat16)
        face_send[h, o, 1] = field[h, o, pl.ds(LOW, LOW), :].astype(jnp.bfloat16)
        for y in range(16):
            layer = field[h, o, pl.ds(LOW + y, 16, stride=16), :]
            turned[o, pl.ds(LOW + 16 * y, 16), :] = layer
            if y >= 10:
                face_send[h, o, 2, pl.ds(16 * (y - 10), 16), :] = layer.astype(jnp.bfloat16)
            if y < RADIUS:
                face_send[h, o, 3, pl.ds(16 * y, 16), :] = layer.astype(jnp.bfloat16)
        first_half = field[h, o, pl.ds(LOW, 128), :].astype(jnp.bfloat16)
        second_half = field[h, o, pl.ds(LOW + 128, 128), :].astype(jnp.bfloat16)
        edges = dot_nt(pick_matrix[:, 0:128], first_half) + dot_nt(
            pick_matrix[:, 128:256], second_half
        )
        edge_send[h, o, 0] = edges[0:16].astype(jnp.bfloat16)
        edge_send[h, o, 1] = edges[16:32].astype(jnp.bfloat16)

    def project(batch, h, orbs):
        def body(x, sums):
            sums = list(sums)
            for y in range(16):
                row = x * 16 + y
                columns = proj[:, pl.ds(pl.multiple_of(row * 128, 128), 128)]
                for i, o in enumerate(orbs):
                    sums[i] = sums[i] + columns * field[h, o, pl.ds(LOW + row, 1), :]
            return tuple(sums)

        zero = jnp.zeros((SLOTS, 128), jnp.float32)
        sums = lax.fori_loop(0, 16, body, (zero,) * len(orbs))
        chosen = selector[...]
        if len(orbs) < ORBS:
            coef_send[batch, 0] = jnp.zeros((ORBS, 128), jnp.float32)
        for i, o in enumerate(orbs):
            partial = jnp.sum(sums[i], axis=1, keepdims=True)
            coef_send[batch, 0, o : o + 1, :] = jnp.sum(partial * chosen, axis=0, keepdims=True)

    def send_coefficients(batch, turn):
        for k in range(6):
            coef_copy(batch, turn, k).start()

    def own_coefficients(batch):
        for k in range(6):
            coef_copy(batch, 0, k).wait_recv()
        total = pltpu.roll(coef_send[batch, 0], 32, 1)
        for k in range(6):
            total = total + pltpu.roll(coef_recv[batch, 0, k], (128 - 16 * (k ^ 1)) % 128, 1)
        coef_send[batch, 1] = total * own_energy
        send_coefficients(batch, 1)

    def weigh(batch, orbs):
        for k in range(6):
            coef_copy(batch, 1, k).wait_recv()
        known = pltpu.roll(coef_send[batch, 1], 96, 1)
        for k in range(6):
            known = known + pltpu.roll(coef_recv[batch, 1, k], 16 * k, 1)
        chosen = selector[...]
        for o in orbs:
            weight = jnp.sum(chosen * known[o : o + 1, :], axis=1, keepdims=True)
            splat[o * SLOTS : (o + 1) * SLOTS, :] = jnp.broadcast_to(weight, (SLOTS, 128))

    def receive(h, o):
        for k in range(6):
            halo_copy(h, o, k).wait_recv()

    def apply(h, o):
        field[h, o, pl.ds(LOW + CELLROWS, LOW), :] = face_recv[h, o, 0].astype(jnp.float32)
        field[h, o, pl.ds(0, LOW), :] = face_recv[h, o, 1].astype(jnp.float32)
        turned[o, pl.ds(LOW + CELLROWS, LOW), :] = face_recv[h, o, 2].astype(jnp.float32)
        turned[o, pl.ds(0, LOW), :] = face_recv[h, o, 3].astype(jnp.float32)

        high, low = split(field[h, o, pl.ds(LOW, CELLROWS), :])
        along = jnp.dot(
            jnp.concatenate([high, low], axis=1),
            band_matrix[...],
            preferred_element_type=jnp.float32,
        )
        along = along[:, 0:128] + along[:, 128:256]
        ends = dot_tn(
            jnp.concatenate([edge_recv[h, o, 1], edge_recv[h, o, 0]], axis=0), edge_matrix[...]
        )
        term_z[0:128, :] = along[0:128] + (ends[:, 0:128] + ends[:, 128:256])
        term_z[128:256, :] = along[128:256] + (ends[:, 256:384] + ends[:, 384:512])

        def body_y(y, carry):
            total = jnp.zeros((64, 128), jnp.float32)
            for k in range(1, RADIUS + 1):
                total = total + COEF[k] * (
                    turned[o, pl.ds(LOW + 64 * y + 16 * k, 64), :]
                    + turned[o, pl.ds(LOW + 64 * y - 16 * k, 64), :]
                )
            term_y[pl.ds(64 * y, 64), :] = total
            return carry

        lax.fori_loop(0, 4, body_y, 0)

        def body_x(x, carry):
            here = pl.ds(64 * x, 64)
            value = field[h, o, pl.ds(LOW + 64 * x, 64), :]
            total = diag[here, :] * value + term_z[here, :]
            total = total + jnp.concatenate(
                [term_y[pl.ds(4 * x + i, 16, stride=16), :] for i in range(4)], axis=0
            )
            for k in range(1, RADIUS + 1):
                total = total + COEF[k] * (
                    field[h, o, pl.ds(LOW + 64 * x + 16 * k, 64), :]
                    + field[h, o, pl.ds(LOW + 64 * x - 16 * k, 64), :]
                )
            for s in range(SLOTS):
                total = total + splat[pl.ds(o * SLOTS + s, 1), :] * proj_rows[
                    pl.ds(s * CELLROWS + 64 * x, 64), :
                ]
            if h == 0:
                field[1, o, pl.ds(LOW + 64 * x, 64), :] = total
            else:
                total = 2.0 * total - field[0, o, pl.ds(LOW + 64 * x, 64), :]
                place = pl.ds(o * CELLROWS + 64 * x, 64)
                filtered[place, :] = total
                for i in range(4):
                    rounded[o, 4 * x + i] = total[16 * i : 16 * i + 16].astype(jnp.bfloat16)
            return carry

        lax.fori_loop(0, 4, body_x, 0)

    def part_of(part):
        return (0, 2) if part == 0 else (part + 1, 1)

    def result_copy(part):
        first, many = part_of(part)
        place = pl.ds(first * CELLROWS, many * CELLROWS)
        return pltpu.make_async_copy(filtered.at[place], filt_hbm.at[place], out_sem.at[part])

    def cell_copy(part, i):
        orbs = pl.ds(*part_of(part))
        return pltpu.make_async_remote_copy(
            src_ref=rounded.at[orbs, band_peer(i)],
            dst_ref=cells.at[b, orbs],
            send_sem=cell_send_sem.at[part, i],
            recv_sem=cell_recv_sem.at[part, i],
            device_id=(d, band_peer(i)),
            device_id_type=MESH,
        )

    def publish(part):
        each(1, BANDS, lambda i: cell_copy(part, i).start())
        result_copy(part).start()

    def share_copy(i):
        return pltpu.make_async_remote_copy(
            src_ref=shares.at[band_peer(i)],
            dst_ref=gathered.at[b],
            send_sem=share_send_sem.at[i],
            recv_sem=share_recv_sem.at[i],
            device_id=(d, band_peer(i)),
            device_id_type=MESH,
        )

    def low_copy(i):
        return pltpu.make_async_remote_copy(
            src_ref=group_low.at[d_low],
            dst_ref=group_low.at[d_low],
            send_sem=low_send_sem.at[i],
            recv_sem=low_recv_sem.at[i],
            device_id=(low_peer(i), b),
            device_id_type=MESH,
        )

    def high_copy(i):
        return pltpu.make_async_remote_copy(
            src_ref=group_high.at[d_high],
            dst_ref=group_high.at[d_high],
            send_sem=high_send_sem.at[i],
            recv_sem=high_recv_sem.at[i],
            device_id=(high_peer(i), b),
            device_id_type=MESH,
        )

    for o in range(ORBS):
        loads[o].wait()
    each(0, ORBS, lambda o: prepare(0, o))
    loads[ORBS].wait()
    project(0, 0, (0, 1, 2, 3))
    pl.semaphore_wait(barrier, 14 + BANDS - 1)
    send_coefficients(0, 0)
    send_halo(0, 0)
    def turn(row, carry):
        proj_rows[pl.ds(row, SLOTS, stride=CELLROWS), :] = proj[
            :, pl.ds(pl.multiple_of(row * 128, 128), 128)
        ]
        return carry

    lax.fori_loop(0, CELLROWS, turn, 0, unroll=8)
    loads[ORBS + 1].wait()
    diag[...] = (diag[...] + (-0.5 / (SPACING * SPACING) * 3.0 * STENCIL[0] - CENTER)) * (
        1.0 / HALF_WIDTH
    )
    own_coefficients(0)
    send_halo(0, 1)
    receive(0, 0)
    send_halo(0, 2)
    weigh(0, (0, 1, 2, 3))

    def first_step(o):
        apply(0, o)
        prepare(1, o)

    first_step(0)
    receive(0, 1)
    send_halo(0, 3)
    first_step(1)
    receive(0, 2)
    send_halo(1, 0)
    first_step(2)
    receive(0, 3)
    first_step(3)
    project(1, 1, (0, 1, 2, 3))
    send_coefficients(1, 0)
    send_halo(1, 1)

    receive(1, 0)
    send_halo(1, 2)
    own_coefficients(1)
    receive(1, 1)
    send_halo(1, 3)
    weigh(1, (0, 1, 2, 3))
    apply(1, 0)
    apply(1, 1)
    publish(0)
    receive(1, 2)
    apply(1, 2)
    publish(1)
    receive(1, 3)
    apply(1, 3)
    publish(2)

    cells[b] = rounded[:, b]
    for part in range(3):
        each(1, BANDS, lambda i: cell_copy(part, i).wait_recv())

    def widen(j):
        for o in range(ORBS):
            wide[pl.ds(j * 64 + o * 16, 16), :] = cells[j, o].astype(jnp.float32)

    each(0, BANDS, widen)
    gram = jnp.zeros((64, 64), jnp.float32)
    for row in range(0, 16, 2):
        part = jnp.concatenate(
            [wide[pl.ds(row + i, 64, stride=16), :] for i in range(2)], axis=1
        ).astype(jnp.bfloat16)
        gram = gram + dot_nt(part, part)
    gram = jnp.concatenate([gram, jnp.zeros((64, 64), jnp.float32)], axis=1)
    for j in range(BANDS):
        shares[j] = gram[ORBS * j : ORBS * (j + 1), :]
    each(1, BANDS, lambda i: share_copy(i).start())
    gathered[b] = shares[b]
    each(1, BANDS, lambda i: share_copy(i).wait_recv())
    total = gathered[0]
    for j in range(1, BANDS):
        total = total + gathered[j]
    group_low[d_low] = total
    each(1, 8, lambda i: low_copy(i).start())
    each(1, 8, lambda i: low_copy(i).wait_recv())
    total = group_low[0]
    for j in range(1, 8):
        total = total + group_low[j]
    group_high[d_high] = total
    each(1, 8, lambda i: high_copy(i).start())
    each(1, 8, lambda i: high_copy(i).wait_recv())
    total = group_high[0]
    for j in range(1, 8):
        total = total + group_high[j]
    margin_ref[...] = total[:, 0:64] * (1.0 / NCELLS)

    for batch in range(2):
        for turn_ in range(2):
            for k in range(6):
                coef_copy(batch, turn_, k).wait_send()

    def sent(i):
        for k in range(6):
            halo_copy(i // ORBS, i % ORBS, k).wait_send()

    each(0, 2 * ORBS, sent)
    for part in range(3):
        result_copy(part).wait()
        each(1, BANDS, lambda i: cell_copy(part, i).wait_send())
    each(1, BANDS, lambda i: share_copy(i).wait_send())
    each(1, 8, lambda i: low_copy(i).wait_send())
    each(1, 8, lambda i: high_copy(i).wait_send())


def copy_kernel(filt_in, margin_in, filt_out, margin_out):
    filt_out[...] = filt_in[...]
    margin_out[...] = margin_in[...]


def on_device(orbitals, potential, projectors, slot_ids, slot_count, energies):
    vmem = pl.BlockSpec(memory_space=pltpu.VMEM)
    smem = pl.BlockSpec(memory_space=pltpu.SMEM)
    hbm = pl.BlockSpec(memory_space=pltpu.HBM)
    dma = pltpu.SemaphoreType.DMA
    filtered, margin = pl.pallas_call(
        kernel,
        out_shape=(
            jax.ShapeDtypeStruct((ORBS * CELLROWS, 128), jnp.float32),
            jax.ShapeDtypeStruct((ORBS, 64), jnp.float32),
        ),
        in_specs=[smem, smem] + [hbm] * 4,
        out_specs=(hbm, vmem),
        scratch_shapes=[
            pltpu.VMEM((8, 128), jnp.float32),
            pltpu.VMEM((2, ORBS, PADROWS, 128), jnp.float32),
            pltpu.VMEM((ORBS, PADROWS, 128), jnp.float32),
            pltpu.VMEM((SLOTS, 32768), jnp.float32),
            pltpu.VMEM((SLOTS * CELLROWS, 128), jnp.float32),
            pltpu.VMEM((CELLROWS, 128), jnp.float32),
            pltpu.VMEM((2, ORBS, 4, LOW, 128), jnp.bfloat16),
            pltpu.VMEM((2, ORBS, 4, LOW, 128), jnp.bfloat16),
            pltpu.VMEM((2, ORBS, 2, 16, 128), jnp.bfloat16),
            pltpu.VMEM((2, ORBS, 2, 16, 128), jnp.bfloat16),
            pltpu.VMEM((2, 2, ORBS, 128), jnp.float32),
            pltpu.VMEM((2, 2, 6, ORBS, 128), jnp.float32),
            pltpu.VMEM((256, 256), jnp.bfloat16),
            pltpu.VMEM((32, 512), jnp.bfloat16),
            pltpu.VMEM((32, 256), jnp.bfloat16),
            pltpu.VMEM((SLOTS, 128), jnp.float32),
            pltpu.VMEM((ORBS * SLOTS, 128), jnp.float32),
            pltpu.VMEM((CELLROWS, 128), jnp.float32),
            pltpu.VMEM((CELLROWS, 128), jnp.float32),
            pltpu.VMEM((ORBS * CELLROWS, 128), jnp.float32),
            pltpu.VMEM((ORBS, BANDS, 16, 128), jnp.bfloat16),
            pltpu.VMEM((BANDS, ORBS, 16, 128), jnp.bfloat16),
            pltpu.VMEM((64 * 16, 128), jnp.float32),
            pltpu.VMEM((BANDS, ORBS, 128), jnp.float32),
            pltpu.VMEM((BANDS, ORBS, 128), jnp.float32),
            pltpu.VMEM((8, ORBS, 128), jnp.float32),
            pltpu.VMEM((8, ORBS, 128), jnp.float32),
            dma((ORBS + 3,)),
            dma((3,)),
            dma((2, ORBS, 6)),
            dma((2, ORBS, 6)),
            dma((2, 2, 6)),
            dma((2, 2, 6)),
            dma((3, BANDS)),
            dma((3, BANDS)),
            dma((BANDS,)),
            dma((BANDS,)),
            dma((8,)),
            dma((8,)),
            dma((8,)),
            dma((8,)),
        ],
        compiler_params=pltpu.CompilerParams(
            collective_id=0, has_side_effects=True, vmem_limit_bytes=62 * 2**20
        ),
        name="chebyshev",
    )(
        slot_ids,
        slot_count,
        energies.reshape(8, 128),
        orbitals.reshape(ORBS * CELLROWS, 128),
        potential.reshape(CELLROWS, 128),
        projectors,
    )
    filtered, margin = pl.pallas_call(
        copy_kernel,
        out_shape=(
            jax.ShapeDtypeStruct(filtered.shape, jnp.float32),
            jax.ShapeDtypeStruct(margin.shape, jnp.float32),
        ),
        in_specs=[vmem, vmem],
        out_specs=(vmem, vmem),
        name="results",
    )(filtered, margin)
    return filtered.reshape(orbitals.shape), margin


def solution(mesh):
    in_specs = (
        P("band", "domain", None, None),
        P("domain", None, None),
        P("domain", None),
        P("domain"),
        P("domain"),
        P(),
    )
    out_specs = (P("band", "domain", None, None), P("band", None))
    return jax.shard_map(
        on_device, mesh=mesh, in_specs=in_specs, out_specs=out_specs, check_vma=False
    )
```

```python
import jax
import jax.numpy as jnp
from jax import lax
from jax.experimental import pallas as pl
from jax.experimental.pallas import tpu as pltpu
from jax.sharding import PartitionSpec as P

STENCIL = (
    -5369.0 / 1800.0,
    12.0 / 7.0,
    -15.0 / 56.0,
    10.0 / 189.0,
    -1.0 / 112.0,
    2.0 / 1925.0,
    -1.0 / 16632.0,
)
SPACING = 0.5
CENTER = 27.5
HALF_WIDTH = 22.5
RADIUS = 6
ORBS = 4
SLOTS = 32
CELLROWS = 256
PADROWS = 448
LOW = 96
DOMAINS = 64
BANDS = 16
NCELLS = 2097152

SCALE = -0.5 / (SPACING * SPACING) / HALF_WIDTH
COEF = [SCALE * c for c in STENCIL]
MESH = pl.DeviceIdType.MESH


def neighbours(d):
    found = []
    for low in (16, 4, 1):
        first, second = d // low % 2, d // (2 * low) % 2
        by_first = d + low * (1 - 2 * first)
        by_second = d + 2 * low * (1 - 2 * second)
        lead = 1 - (first + second) % 2
        found.append(lead * by_first + (1 - lead) * by_second)
        found.append(lead * by_second + (1 - lead) * by_first)
    return found


NEAR = (16, 32, 8, 4, 2, 1)
AROUND = (24, 20, 18, 17, 40, 36, 34, 33, 48, 10, 9, 12, 6, 5, 3) + NEAR
OTHERS = tuple(m for m in AROUND if m > 7 and m % 8)


def flip(d, mask):
    for bit in (1, 2, 4, 8, 16, 32):
        if mask & bit:
            d = d + bit * (1 - 2 * (d // bit % 2))
    return d


def split(value):
    high = value.astype(jnp.bfloat16)
    low = (value - high.astype(jnp.float32)).astype(jnp.bfloat16)
    return high, low


def dot_nt(left, right):
    return lax.dot_general(
        left, right, (((1,), (1,)), ((), ())), preferred_element_type=jnp.float32
    )


def dot_tn(left, right):
    return lax.dot_general(
        left, right, (((0,), (0,)), ((), ())), preferred_element_type=jnp.float32
    )


def kernel(
    ids_ref,
    count_ref,
    energies_ref,
    orb_ref,
    pot_ref,
    proj_ref,
    filt_hbm,
    margin_ref,
    field,
    turned,
    proj,
    proj_rows,
    diag,
    face_send,
    face_recv,
    edge_send,
    edge_recv,
    coef_send,
    coef_recv,
    band_matrix,
    edge_matrix,
    pick_matrix,
    down,
    strength,
    splat,
    term_y,
    term_z,
    filtered,
    rounded,
    cells,
    wide,
    shares,
    gathered,
    group_low,
    group_high,
    in_sem,
    out_sem,
    halo_send_sem,
    halo_recv_sem,
    coef_send_sem,
    coef_recv_sem,
    cell_send_sem,
    cell_recv_sem,
    share_send_sem,
    share_recv_sem,
    low_send_sem,
    low_recv_sem,
    high_send_sem,
    high_recv_sem,
):
    d = lax.axis_index("domain")
    b = lax.axis_index("band")
    near = neighbours(d)

    loads = [
        pltpu.make_async_copy(
            orb_ref.at[pl.ds(o * CELLROWS, CELLROWS)],
            field.at[0, o, pl.ds(LOW, CELLROWS)],
            in_sem.at[o],
        )
        for o in range(ORBS)
    ]
    loads.append(pltpu.make_async_copy(proj_ref, proj, in_sem.at[ORBS]))
    loads.append(pltpu.make_async_copy(pot_ref, diag, in_sem.at[ORBS + 1]))

    d_low, d_high = d % 8, d // 8

    def band_peer(i):
        return (b + i) % BANDS

    def low_peer(i):
        return d_high * 8 + (d_low + i) % 8

    def high_peer(i):
        return (d_high + i) % 8 * 8 + d_low

    def each(first, last, body):
        lax.fori_loop(first, last, lambda i, carry: (body(i), carry)[1], 0)

    barrier = pltpu.get_barrier_semaphore()

    def greet_band(i):
        pl.semaphore_signal(barrier, inc=1, device_id=(d, band_peer(i)), device_id_type=MESH)

    def greet_domain(i):
        pl.semaphore_signal(barrier, inc=1, device_id=(high_peer(i), b), device_id_type=MESH)
        pl.semaphore_signal(barrier, inc=1, device_id=(low_peer(i), b), device_id_type=MESH)

    each(1, 8, greet_domain)
    for mask in OTHERS:
        pl.semaphore_signal(barrier, inc=1, device_id=(flip(d, mask), b), device_id_type=MESH)
    each(1, BANDS, greet_band)
    for load in loads:
        load.start()

    rows = lax.broadcasted_iota(jnp.int32, (128, 128), 0)
    lanes = lax.broadcasted_iota(jnp.int32, (128, 128), 1)
    apart = jnp.abs(rows - lanes)
    banded = jnp.zeros((128, 128), jnp.float32)
    for k in range(1, RADIUS + 1):
        banded = jnp.where(apart == k, COEF[k], banded)
    high, low = split(banded)
    band_matrix[0:128, 0:128] = high
    band_matrix[128:256, 0:128] = high
    band_matrix[0:128, 128:256] = low
    band_matrix[128:256, 128:256] = low

    rows = lax.broadcasted_iota(jnp.int32, (32, 128), 0)
    lanes = lax.broadcasted_iota(jnp.int32, (32, 128), 1)
    layer = rows & 7
    half = (rows >> 3) & 1
    side = rows >> 4
    used = layer < RADIUS
    reach = jnp.where(side == 0, lanes + RADIUS - layer, 128 + layer - lanes)
    edge = jnp.zeros((32, 128), jnp.float32)
    for k in range(1, RADIUS + 1):
        edge = jnp.where(reach == k, COEF[k], edge)
    edge = jnp.where(used, edge, 0.0)
    picked = jnp.where(side == 0, 128 - RADIUS + layer, layer)
    pick = jnp.where(used, jnp.where(lanes == picked, 1.0, 0.0), 0.0)
    for part in range(2):
        high, low = split(jnp.where(half == part, edge, 0.0))
        edge_matrix[:, 256 * part : 256 * part + 128] = high
        edge_matrix[:, 256 * part + 128 : 256 * part + 256] = low
        pick_matrix[:, 128 * part : 128 * part + 128] = jnp.where(half == part, pick, 0.0).astype(
            jnp.bfloat16
        )

    lane = lax.broadcasted_iota(jnp.int32, (1, 128), 1)
    live = count_ref[0]
    across = jnp.zeros((1, 128), jnp.float32)
    for s in range(SLOTS):
        name = jnp.where(s < live, ids_ref[s].astype(jnp.float32), -1.0)
        across = jnp.where((lane & 31) == s, name, across)
        down[s : s + 1, :] = jnp.full((1, 128), jnp.where(s < live, name, -2.0))
        strength[s : s + 1, :] = jnp.full((1, 128), energies_ref[ids_ref[s]] * (1.0 / HALF_WIDTH))
    coef_send[0, 1:2, :] = across
    coef_send[1, 1:2, :] = across
    living = jnp.where((lane & 31) < live, 1.0, 0.0)

    def halo_copy(h, o, k):
        if k < 4:
            src, dst = face_send.at[h, o, k], face_recv.at[h, o, k ^ 1]
        else:
            src, dst = edge_send.at[h, o, k - 4], edge_recv.at[h, o, (k ^ 1) - 4]
        return pltpu.make_async_remote_copy(
            src_ref=src,
            dst_ref=dst,
            send_sem=halo_send_sem.at[h, o, k],
            recv_sem=halo_recv_sem.at[h, o, k ^ 1],
            device_id=(near[k], b),
            device_id_type=MESH,
        )

    def send_halo(h, o):
        for k in range(6):
            halo_copy(h, o, k).start()

    def coef_copy(h, j):
        return pltpu.make_async_remote_copy(
            src_ref=coef_send.at[h],
            dst_ref=coef_recv.at[h, j],
            send_sem=coef_send_sem.at[h, j],
            recv_sem=coef_recv_sem.at[h, j],
            device_id=(flip(d, AROUND[j]), b),
            device_id_type=MESH,
        )

    def prepare(h, o):
        face_send[h, o, 0] = field[h, o, pl.ds(LOW + 160, LOW), :].astype(jnp.bfloat16)
        face_send[h, o, 1] = field[h, o, pl.ds(LOW, LOW), :].astype(jnp.bfloat16)
        for y in range(16):
            layer = field[h, o, pl.ds(LOW + y, 16, stride=16), :]
            turned[o, pl.ds(LOW + 16 * y, 16), :] = layer
            if y >= 10:
                face_send[h, o, 2, pl.ds(16 * (y - 10), 16), :] = layer.astype(jnp.bfloat16)
            if y < RADIUS:
                face_send[h, o, 3, pl.ds(16 * y, 16), :] = layer.astype(jnp.bfloat16)
        first_half = field[h, o, pl.ds(LOW, 128), :].astype(jnp.bfloat16)
        second_half = field[h, o, pl.ds(LOW + 128, 128), :].astype(jnp.bfloat16)
        edges = dot_nt(pick_matrix[:, 0:128], first_half) + dot_nt(
            pick_matrix[:, 128:256], second_half
        )
        edge_send[h, o, 0] = edges[0:16].astype(jnp.bfloat16)
        edge_send[h, o, 1] = edges[16:32].astype(jnp.bfloat16)

    def project(h):
        def body(x, sums):
            sums = list(sums)
            for y in range(16):
                row = x * 16 + y
                columns = proj[:, pl.ds(pl.multiple_of(row * 128, 128), 128)]
                for o in range(ORBS):
                    sums[o] = sums[o] + columns * field[h, o, pl.ds(LOW + row, 1), :]
            return tuple(sums)

        zero = jnp.zeros((SLOTS, 128), jnp.float32)
        sums = lax.fori_loop(0, 16, body, (zero,) * ORBS)
        slot = lax.broadcasted_iota(jnp.int32, (SLOTS, 128), 0)
        place = lax.broadcasted_iota(jnp.int32, (SLOTS, 128), 1)
        laid = zero
        for o in range(ORBS):
            partial = jnp.sum(sums[o], axis=1, keepdims=True)
            laid = jnp.where(place == slot + SLOTS * o, partial, laid)
        coef_send[h, 0:1, :] = jnp.sum(laid, axis=0, keepdims=True) * living

    def send_coefficients(h):
        for j in range(len(AROUND)):
            coef_copy(h, j).start()

    def weigh(h):
        for j in range(len(AROUND)):
            coef_copy(h, j).wait_recv()
        names = down[...]
        found = jnp.where(names == coef_send[h, 1:2, :], coef_send[h, 0:1, :], 0.0)
        for j in range(len(AROUND)):
            found = found + jnp.where(
                names == coef_recv[h, j, 1:2, :], coef_recv[h, j, 0:1, :], 0.0
            )
        found = found * strength[...]
        place = lax.broadcasted_iota(jnp.int32, (SLOTS, 128), 1)
        for o in range(ORBS):
            mine = jnp.where((place >> 5) == o, found, 0.0)
            weight = jnp.sum(mine, axis=1, keepdims=True)
            splat[o * SLOTS : (o + 1) * SLOTS, :] = jnp.broadcast_to(weight, (SLOTS, 128))

    def receive(h, o):
        for k in range(6):
            halo_copy(h, o, k).wait_recv()

    def apply(h, o):
        field[h, o, pl.ds(LOW + CELLROWS, LOW), :] = face_recv[h, o, 0].astype(jnp.float32)
        field[h, o, pl.ds(0, LOW), :] = face_recv[h, o, 1].astype(jnp.float32)
        turned[o, pl.ds(LOW + CELLROWS, LOW), :] = face_recv[h, o, 2].astype(jnp.float32)
        turned[o, pl.ds(0, LOW), :] = face_recv[h, o, 3].astype(jnp.float32)

        high, low = split(field[h, o, pl.ds(LOW, CELLROWS), :])
        along = jnp.dot(
            jnp.concatenate([high, low], axis=1),
            band_matrix[...],
            preferred_element_type=jnp.float32,
        )
        along = along[:, 0:128] + along[:, 128:256]
        ends = dot_tn(
            jnp.concatenate([edge_recv[h, o, 1], edge_recv[h, o, 0]], axis=0), edge_matrix[...]
        )
        term_z[0:128, :] = along[0:128] + (ends[:, 0:128] + ends[:, 128:256])
        term_z[128:256, :] = along[128:256] + (ends[:, 256:384] + ends[:, 384:512])

        def body_y(y, carry):
            total = jnp.zeros((64, 128), jnp.float32)
            for k in range(1, RADIUS + 1):
                total = total + COEF[k] * (
                    turned[o, pl.ds(LOW + 64 * y + 16 * k, 64), :]
                    + turned[o, pl.ds(LOW + 64 * y - 16 * k, 64), :]
                )
            term_y[pl.ds(64 * y, 64), :] = total
            return carry

        lax.fori_loop(0, 4, body_y, 0)

        def body_x(x, carry):
            here = pl.ds(64 * x, 64)
            value = field[h, o, pl.ds(LOW + 64 * x, 64), :]
            total = diag[here, :] * value + term_z[here, :]
            total = total + jnp.concatenate(
                [term_y[pl.ds(4 * x + i, 16, stride=16), :] for i in range(4)], axis=0
            )
            for k in range(1, RADIUS + 1):
                total = total + COEF[k] * (
                    field[h, o, pl.ds(LOW + 64 * x + 16 * k, 64), :]
                    + field[h, o, pl.ds(LOW + 64 * x - 16 * k, 64), :]
                )
            for s in range(SLOTS):
                total = total + splat[pl.ds(o * SLOTS + s, 1), :] * proj_rows[
                    pl.ds(s * CELLROWS + 64 * x, 64), :
                ]
            if h == 0:
                field[1, o, pl.ds(LOW + 64 * x, 64), :] = total
            else:
                total = 2.0 * total - field[0, o, pl.ds(LOW + 64 * x, 64), :]
                place = pl.ds(o * CELLROWS + 64 * x, 64)
                filtered[place, :] = total
                for i in range(4):
                    rounded[o, 4 * x + i] = total[16 * i : 16 * i + 16].astype(jnp.bfloat16)
            return carry

        lax.fori_loop(0, 4, body_x, 0)

    def part_of(part):
        return (0, 2) if part == 0 else (part + 1, 1)

    def result_copy(part):
        first, many = part_of(part)
        place = pl.ds(first * CELLROWS, many * CELLROWS)
        return pltpu.make_async_copy(filtered.at[place], filt_hbm.at[place], out_sem.at[part])

    def cell_copy(part, i):
        orbs = pl.ds(*part_of(part))
        return pltpu.make_async_remote_copy(
            src_ref=rounded.at[orbs, band_peer(i)],
            dst_ref=cells.at[b, orbs],
            send_sem=cell_send_sem.at[part, i],
            recv_sem=cell_recv_sem.at[part, i],
            device_id=(d, band_peer(i)),
            device_id_type=MESH,
        )

    def publish(part):
        each(1, BANDS, lambda i: cell_copy(part, i).start())
        result_copy(part).start()

    def share_copy(i):
        return pltpu.make_async_remote_copy(
            src_ref=shares.at[band_peer(i)],
            dst_ref=gathered.at[b],
            send_sem=share_send_sem.at[i],
            recv_sem=share_recv_sem.at[i],
            device_id=(d, band_peer(i)),
            device_id_type=MESH,
        )

    def low_copy(i):
        return pltpu.make_async_remote_copy(
            src_ref=group_low.at[d_low],
            dst_ref=group_low.at[d_low],
            send_sem=low_send_sem.at[i],
            recv_sem=low_recv_sem.at[i],
            device_id=(low_peer(i), b),
            device_id_type=MESH,
        )

    def high_copy(i):
        return pltpu.make_async_remote_copy(
            src_ref=group_high.at[d_high],
            dst_ref=group_high.at[d_high],
            send_sem=high_send_sem.at[i],
            recv_sem=high_recv_sem.at[i],
            device_id=(high_peer(i), b),
            device_id_type=MESH,
        )

    for o in range(ORBS):
        loads[o].wait()
    each(0, ORBS, lambda o: prepare(0, o))
    loads[ORBS].wait()
    project(0)
    pl.semaphore_wait(barrier, 14 + len(OTHERS) + BANDS - 1)
    send_coefficients(0)
    send_halo(0, 0)
    send_halo(0, 1)

    def turn(row, carry):
        proj_rows[pl.ds(row, SLOTS, stride=CELLROWS), :] = proj[
            :, pl.ds(pl.multiple_of(row * 128, 128), 128)
        ]
        return carry

    lax.fori_loop(0, CELLROWS, turn, 0, unroll=8)
    loads[ORBS + 1].wait()
    diag[...] = (diag[...] + (-0.5 / (SPACING * SPACING) * 3.0 * STENCIL[0] - CENTER)) * (
        1.0 / HALF_WIDTH
    )
    receive(0, 0)
    send_halo(0, 2)
    weigh(0)

    def first_step(o):
        apply(0, o)
        prepare(1, o)

    first_step(0)
    receive(0, 1)
    send_halo(0, 3)
    first_step(1)
    send_halo(1, 0)
    receive(0, 2)
    first_step(2)
    send_halo(1, 1)
    receive(0, 3)
    first_step(3)
    project(1)
    send_coefficients(1)
    send_halo(1, 2)

    receive(1, 0)
    send_halo(1, 3)
    receive(1, 1)
    weigh(1)
    apply(1, 0)
    apply(1, 1)
    publish(0)
    receive(1, 2)
    apply(1, 2)
    publish(1)
    receive(1, 3)
    apply(1, 3)
    publish(2)

    cells[b] = rounded[:, b]
    for part in range(3):
        each(1, BANDS, lambda i: cell_copy(part, i).wait_recv())

    def widen(j):
        for o in range(ORBS):
            wide[pl.ds(j * 64 + o * 16, 16), :] = cells[j, o].astype(jnp.float32)

    each(0, BANDS, widen)
    gram = jnp.zeros((64, 64), jnp.float32)
    for row in range(0, 16, 2):
        part = jnp.concatenate(
            [wide[pl.ds(row + i, 64, stride=16), :] for i in range(2)], axis=1
        ).astype(jnp.bfloat16)
        gram = gram + dot_nt(part, part)
    gram = jnp.concatenate([gram, jnp.zeros((64, 64), jnp.float32)], axis=1)
    for j in range(BANDS):
        shares[j] = gram[ORBS * j : ORBS * (j + 1), :]
    each(1, BANDS, lambda i: share_copy(i).start())
    gathered[b] = shares[b]
    each(1, BANDS, lambda i: share_copy(i).wait_recv())
    total = gathered[0]
    for j in range(1, BANDS):
        total = total + gathered[j]
    group_low[d_low] = total
    each(1, 8, lambda i: low_copy(i).start())
    each(1, 8, lambda i: low_copy(i).wait_recv())
    total = group_low[0]
    for j in range(1, 8):
        total = total + group_low[j]
    group_high[d_high] = total
    each(1, 8, lambda i: high_copy(i).start())
    each(1, 8, lambda i: high_copy(i).wait_recv())
    total = group_high[0]
    for j in range(1, 8):
        total = total + group_high[j]
    margin_ref[...] = total[:, 0:64] * (1.0 / NCELLS)

    for h in range(2):
        for j in range(len(AROUND)):
            coef_copy(h, j).wait_send()

    def sent(i):
        for k in range(6):
            halo_copy(i // ORBS, i % ORBS, k).wait_send()

    each(0, 2 * ORBS, sent)
    for part in range(3):
        result_copy(part).wait()
        each(1, BANDS, lambda i: cell_copy(part, i).wait_send())
    each(1, BANDS, lambda i: share_copy(i).wait_send())
    each(1, 8, lambda i: low_copy(i).wait_send())
    each(1, 8, lambda i: high_copy(i).wait_send())


def copy_kernel(filt_in, margin_in, filt_out, margin_out):
    filt_out[...] = filt_in[...]
    margin_out[...] = margin_in[...]


def on_device(orbitals, potential, projectors, slot_ids, slot_count, energies):
    vmem = pl.BlockSpec(memory_space=pltpu.VMEM)
    smem = pl.BlockSpec(memory_space=pltpu.SMEM)
    hbm = pl.BlockSpec(memory_space=pltpu.HBM)
    dma = pltpu.SemaphoreType.DMA
    filtered, margin = pl.pallas_call(
        kernel,
        out_shape=(
            jax.ShapeDtypeStruct((ORBS * CELLROWS, 128), jnp.float32),
            jax.ShapeDtypeStruct((ORBS, 64), jnp.float32),
        ),
        in_specs=[smem, smem, smem] + [hbm] * 3,
        out_specs=(hbm, vmem),
        scratch_shapes=[
            pltpu.VMEM((2, ORBS, PADROWS, 128), jnp.float32),
            pltpu.VMEM((ORBS, PADROWS, 128), jnp.float32),
            pltpu.VMEM((SLOTS, 32768), jnp.float32),
            pltpu.VMEM((SLOTS * CELLROWS, 128), jnp.float32),
            pltpu.VMEM((CELLROWS, 128), jnp.float32),
            pltpu.VMEM((2, ORBS, 4, LOW, 128), jnp.bfloat16),
            pltpu.VMEM((2, ORBS, 4, LOW, 128), jnp.bfloat16),
            pltpu.VMEM((2, ORBS, 2, 16, 128), jnp.bfloat16),
            pltpu.VMEM((2, ORBS, 2, 16, 128), jnp.bfloat16),
            pltpu.VMEM((2, 2, 128), jnp.float32),
            pltpu.VMEM((2, len(AROUND), 2, 128), jnp.float32),
            pltpu.VMEM((256, 256), jnp.bfloat16),
            pltpu.VMEM((32, 512), jnp.bfloat16),
            pltpu.VMEM((32, 256), jnp.bfloat16),
            pltpu.VMEM((SLOTS, 128), jnp.float32),
            pltpu.VMEM((SLOTS, 128), jnp.float32),
            pltpu.VMEM((ORBS * SLOTS, 128), jnp.float32),
            pltpu.VMEM((CELLROWS, 128), jnp.float32),
            pltpu.VMEM((CELLROWS, 128), jnp.float32),
            pltpu.VMEM((ORBS * CELLROWS, 128), jnp.float32),
            pltpu.VMEM((ORBS, BANDS, 16, 128), jnp.bfloat16),
            pltpu.VMEM((BANDS, ORBS, 16, 128), jnp.bfloat16),
            pltpu.VMEM((64 * 16, 128), jnp.float32),
            pltpu.VMEM((BANDS, ORBS, 128), jnp.float32),
            pltpu.VMEM((BANDS, ORBS, 128), jnp.float32),
            pltpu.VMEM((8, ORBS, 128), jnp.float32),
            pltpu.VMEM((8, ORBS, 128), jnp.float32),
            dma((ORBS + 2,)),
            dma((3,)),
            dma((2, ORBS, 6)),
            dma((2, ORBS, 6)),
            dma((2, len(AROUND))),
            dma((2, len(AROUND))),
            dma((3, BANDS)),
            dma((3, BANDS)),
            dma((BANDS,)),
            dma((BANDS,)),
            dma((8,)),
            dma((8,)),
            dma((8,)),
            dma((8,)),
        ],
        compiler_params=pltpu.CompilerParams(
            collective_id=0, has_side_effects=True, vmem_limit_bytes=62 * 2**20
        ),
        name="chebyshev",
    )(
        slot_ids,
        slot_count,
        energies,
        orbitals.reshape(ORBS * CELLROWS, 128),
        potential.reshape(CELLROWS, 128),
        projectors,
    )
    filtered, margin = pl.pallas_call(
        copy_kernel,
        out_shape=(
            jax.ShapeDtypeStruct(filtered.shape, jnp.float32),
            jax.ShapeDtypeStruct(margin.shape, jnp.float32),
        ),
        in_specs=[vmem, vmem],
        out_specs=(vmem, vmem),
        name="results",
    )(filtered, margin)
    return filtered.reshape(orbitals.shape), margin


def solution(mesh):
    in_specs = (
        P("band", "domain", None, None),
        P("domain", None, None),
        P("domain", None),
        P("domain"),
        P("domain"),
        P(),
    )
    out_specs = (P("band", "domain", None, None), P("band", None))
    return jax.shard_map(
        on_device, mesh=mesh, in_specs=in_specs, out_specs=out_specs, check_vma=False
    )
```
